32 devices in a mesh: groups: 2 (over x), pair: 16 (over z, y, core).
Axes of the slice: x: 2, y: 2, z: 4, core: 2. Of those that a mesh axis runs over, the one named last changes fastest.
Arguments:
- chol: bfloat16 [2048, 262144], P('groups', 'pair'), parts along dimension 0, may hold values from -0.3125 to 0.3125
- walkers: bfloat16 [64, 512, 128], P(('groups', 'pair')), parts along dimension 0, may hold values from -6 to 6
- trial: bfloat16 [1024, 128], P('groups'), parts along dimension 0, may hold values from -0.5 to 0.5
- one_body: bfloat16 [1024, 512], P('groups'), parts along dimension 0, may hold values from -0.625 to 0.625
- fields: float32 [64, 1024], P(('groups', 'pair')), parts along dimension 0, may hold values from -6 to 6
- src_shift: int32 [64], P(('groups', 'pair')), parts along dimension 0, may hold values from -1 to 1
- src_slot: int32 [64], P(('groups', 'pair')), parts along dimension 0, may hold values from 0 to 1
Outputs:
- next_walkers: bfloat16 [64, 512, 128], P(('groups', 'pair')), parts along dimension 0
The draws below stay inside these ranges and needn't reach their ends.
There are 2 independent parts, one for each index of `groups`. The reference program is written for one: setup_inputs(seed, part) draws one part's arguments, and reference() takes and returns one part's arrays. A program takes and returns all parts, laid end to end along the dimension named above; each array names one. Nothing has to cross between parts.
All inputs are finite; a program needn't handle non-finite values.
Results may differ from the reference program's by a relative error of at most 0.012.
Values may be sent and summed in bfloat16 or wider, within the bound.
A program may use at most 64 MiB of HBM per device.

```python
import jax
import jax.numpy as jnp
from jax import lax

N = 512
NOCC = 128
NG = 1024
TERMS = 6
W_DEV = 2
WALKERS = 32
PAIRS = 262144
N_PAIR = 16


def set_ends(values, key, low, largest):
    place = [jax.random.randint(jax.random.fold_in(key, axis), (), 0, length) for axis, length in enumerate(values.shape)]
    longest = values.shape.index(max(values.shape))
    beside = place[:longest] + [(place[longest] + 1) % values.shape[longest]] + place[longest + 1:]
    return values.at[tuple(place)].set(low).at[tuple(beside)].set(largest)


def block_levels(rng, extent, cuts, smallest, top_value):
    def one(dim, shards_of):
        steps = jax.random.uniform(jax.random.fold_in(jax.random.fold_in(rng, 6), dim), (shards_of,), jnp.float32, smallest / len(cuts), top_value / len(cuts))
        return jnp.repeat(jnp.exp(steps), extent[dim] // shards_of).reshape((-1,) + (1,) * (len(extent) - dim - 1))

    loudness = one(*cuts[0])
    for cut in cuts[1:]:
        loudness = loudness * one(*cut)
    return loudness


def centred(stream_key, shape, deviation, reach, split=(), held_as=jnp.bfloat16):
    level = block_levels(stream_key, shape, split, -0.22, 0.18) if split else 1.0
    values = jax.random.normal(stream_key, shape, jnp.float32) * deviation * level
    return jnp.minimum(jnp.maximum(values, -reach), reach).astype(held_as)


def setup_inputs(seed: int = 0, part: int = 0) -> dict:
    key_of = jax.random.split(jax.random.key(seed), 8)
    part_keys = jax.random.split(jax.random.fold_in(key_of[7], part), 8)
    return {
        "chol": centred(part_keys[0], (NG, PAIRS), (10.0 / N), 0.3125, ((1, 16),)),
        "walkers": centred(part_keys[1], (WALKERS, N, NOCC), 1.0, 6.0, ((0, 16),)),
        "trial": centred(part_keys[2], (N, NOCC), NOCC ** -0.5, 0.5),
        "one_body": centred(part_keys[3], (N, N), (0.9 / N ** 0.5), 0.625),
        "fields": centred(part_keys[4], (WALKERS, NG), 1.0, 6.0, ((0, 16),), jnp.float32),
        "src_shift": set_ends(jax.random.randint(part_keys[5], (WALKERS,), -1, 2), jax.random.fold_in(part_keys[5], 1), -1, 1).astype(jnp.int32),
        "src_slot": set_ends(jax.random.randint(part_keys[6], (WALKERS,), 0, W_DEV), jax.random.fold_in(part_keys[6], 1), 0, W_DEV - 1).astype(jnp.int32),
    }


sqrt_tau = 0.1
bias_cap = 1.0

def taylor(amat, block):
    a_full = amat.astype(jnp.float32)
    term = block
    total = block.astype(jnp.float32)
    for order in range(1, TERMS):
        product = jnp.einsum('wik,wka->wia', a_full, term.astype(jnp.float32)) / order
        total = total + product
        term = product.astype(jnp.bfloat16)
    return total.astype(jnp.bfloat16)

def reference(chol, walkers, trial, one_body, fields, src_shift, src_slot):
    chol_full = chol.astype(jnp.float32)
    trial_full = trial.astype(jnp.float32)
    blocks = walkers.reshape(N_PAIR, W_DEV, N, NOCC)

    def bias_block(block):
        green = jnp.einsum('wia,ka->wik', block.astype(jnp.float32), trial_full).astype(jnp.bfloat16)
        green = green.reshape(W_DEV, N * N).astype(jnp.float32)
        return lax.dot_general(green, chol_full, (((1,), (1,)), ((), ())))
    force = sqrt_tau * lax.map(bias_block, blocks).reshape(WALKERS, NG)
    shift = (fields - jnp.clip(force, -bias_cap, bias_cap)).astype(jnp.bfloat16)
    shift_blocks = shift.reshape(N_PAIR, W_DEV, NG)
    body_term = one_body.astype(jnp.float32)

    def propagate(pieces):
        shift_part, block = pieces
        potential = (sqrt_tau * jnp.dot(shift_part.astype(jnp.float32), chol_full)).astype(jnp.bfloat16)
        amat = (potential.astype(jnp.float32).reshape(W_DEV, N, N) + body_term).astype(jnp.bfloat16)
        return taylor(amat, block)
    propagated = lax.map(propagate, (shift_blocks, blocks)).reshape(WALKERS, N, NOCC)
    owner = jnp.arange(WALKERS, dtype=jnp.int32) // W_DEV
    source = ((owner + src_shift) % N_PAIR * W_DEV + src_slot).astype(jnp.int32)
    return jnp.take(propagated, source, axis=0)
```

```python
import jax
import jax.numpy as jnp
from jax import lax
from jax.sharding import PartitionSpec as P

TERMS = 6


sqrt_tau = 0.1
bias_cap = 1.0


def padded_2(block, sides, width):
    for axis, dim in sides:
        count = lax.axis_size(axis)
        forward = [(i, i + 1) for i in range(count - 1)]
        forward.append((count - 1, 0))
        backward = [(target, source) for source, target in forward]
        low = lax.ppermute(
            lax.slice_in_dim(block, block.shape[dim] - width, None, axis=dim), axis, forward
        )
        high = lax.ppermute(lax.slice_in_dim(block, 0, width, axis=dim), axis, backward)
        block = jnp.concatenate([low, block, high], axis=dim)
    return block


def taylor(amat, block):
    term = block
    total = block.astype(jnp.float32)
    for order in range(1, TERMS):
        product = jnp.einsum("wik,wka->wia", amat, term, preferred_element_type=jnp.float32) / order
        total = total + product
        term = product.astype(jnp.bfloat16)
    return total.astype(jnp.bfloat16)


def shards(chol, walkers, trial, one_body, fields, src_shift, src_slot):
    w_local, orbitals, _ = walkers.shape
    count = lax.axis_size("pair")
    me = lax.axis_index("pair")
    moved = lax.all_to_all(walkers, "pair", split_axis=1, concat_axis=0, tiled=True)
    source = (me + src_shift + count) % count * w_local + src_slot
    sources = lax.all_gather(source, "pair", axis=0, tiled=True)
    padded = padded_2(walkers, (("pair", 0),), w_local)
    parents = jnp.take(padded, (src_shift + 1) * w_local + src_slot, axis=0)
    formed = jnp.einsum("wia,ka->wik", moved, trial, preferred_element_type=jnp.float32)
    green_rows = formed.astype(jnp.bfloat16).reshape(moved.shape[0], moved.shape[1] * orbitals)
    partial_bias = lax.dot_general(
        green_rows, chol, (((1,), (1,)), ((), ())), preferred_element_type=jnp.float32
    )
    pieces = lax.all_to_all(
        partial_bias.reshape(count, w_local, -1), "pair", split_axis=0, concat_axis=0, tiled=True
    )
    summed = jnp.sum(pieces, axis=0)
    shift = (fields - jnp.clip(sqrt_tau * summed, -bias_cap, bias_cap)).astype(jnp.bfloat16)
    spread = jnp.broadcast_to(shift[None], (count,) + shift.shape)
    every_shift = lax.all_to_all(spread, "pair", split_axis=0, concat_axis=0, tiled=True)
    chosen = jnp.take(every_shift.reshape(count * w_local, -1), sources, axis=0)
    local_potential = (sqrt_tau * jnp.dot(chosen, chol, preferred_element_type=jnp.float32)).astype(
        jnp.bfloat16
    )
    own_potential = lax.all_to_all(local_potential, "pair", split_axis=0, concat_axis=1, tiled=True)
    amat = own_potential.astype(jnp.float32).reshape(w_local, orbitals, orbitals) + one_body.astype(
        jnp.float32
    )
    return taylor(amat.astype(jnp.bfloat16), parents)


def solution(mesh):
    placed = (
        P("groups", "pair"),
        P(("groups", "pair"), None, None),
        P("groups", None),
        P("groups", None),
        P(("groups", "pair"), None),
        P(("groups", "pair")),
        P(("groups", "pair")),
    )
    return jax.shard_map(
        shards,
        mesh=mesh,
        in_specs=placed,
        out_specs=P(("groups", "pair"), None, None),
        check_vma=False,
    )
```

```python
import functools

import jax
import jax.numpy as jnp
from jax import lax
from jax.experimental import pallas as pl
from jax.experimental.pallas import tpu as pltpu
from jax.sharding import PartitionSpec as P

TERMS = 6


sqrt_tau = 0.1
bias_cap = 1.0


def padded_2(block, sides, width):
    for axis, dim in sides:
        count = lax.axis_size(axis)
        forward = [(i, i + 1) for i in range(count - 1)]
        forward.append((count - 1, 0))
        backward = [(target, source) for source, target in forward]
        low = lax.ppermute(
            lax.slice_in_dim(block, block.shape[dim] - width, None, axis=dim), axis, forward
        )
        high = lax.ppermute(lax.slice_in_dim(block, 0, width, axis=dim), axis, backward)
        block = jnp.concatenate([low, block, high], axis=dim)
    return block


def taylor(amat, block):
    term = block
    total = block.astype(jnp.float32)
    for order in range(1, TERMS):
        product = jnp.einsum("wik,wka->wia", amat, term, preferred_element_type=jnp.float32) / order
        total = total + product
        term = product.astype(jnp.bfloat16)
    return total.astype(jnp.bfloat16)


def plain_shards(chol, walkers, trial, one_body, fields, src_shift, src_slot):
    w_local, orbitals, _ = walkers.shape
    count = lax.axis_size("pair")
    me = lax.axis_index("pair")
    moved = lax.all_to_all(walkers, "pair", split_axis=1, concat_axis=0, tiled=True)
    source = (me + src_shift + count) % count * w_local + src_slot
    sources = lax.all_gather(source, "pair", axis=0, tiled=True)
    padded = padded_2(walkers, (("pair", 0),), w_local)
    parents = jnp.take(padded, (src_shift + 1) * w_local + src_slot, axis=0)
    formed = jnp.einsum("wia,ka->wik", moved, trial, preferred_element_type=jnp.float32)
    green_rows = formed.astype(jnp.bfloat16).reshape(moved.shape[0], moved.shape[1] * orbitals)
    partial_bias = lax.dot_general(
        green_rows, chol, (((1,), (1,)), ((), ())), preferred_element_type=jnp.float32
    )
    pieces = lax.all_to_all(
        partial_bias.reshape(count, w_local, -1), "pair", split_axis=0, concat_axis=0, tiled=True
    )
    summed = jnp.sum(pieces, axis=0)
    shift = (fields - jnp.clip(sqrt_tau * summed, -bias_cap, bias_cap)).astype(jnp.bfloat16)
    spread = jnp.broadcast_to(shift[None], (count,) + shift.shape)
    every_shift = lax.all_to_all(spread, "pair", split_axis=0, concat_axis=0, tiled=True)
    chosen = jnp.take(every_shift.reshape(count * w_local, -1), sources, axis=0)
    local_potential = (sqrt_tau * jnp.dot(chosen, chol, preferred_element_type=jnp.float32)).astype(
        jnp.bfloat16
    )
    own_potential = lax.all_to_all(local_potential, "pair", split_axis=0, concat_axis=1, tiled=True)
    amat = own_potential.astype(jnp.float32).reshape(w_local, orbitals, orbitals) + one_body.astype(
        jnp.float32
    )
    return taylor(amat.astype(jnp.bfloat16), parents)


MESH = pl.DeviceIdType.MESH


def step_kernel(
    count, chunks,
    chol, walkers, trial, one_body, fields, onehot, weights, out,
    held, rows_in, halo, green, picks_in, bias_out, bias_in, shift_in, flat, picks,
    chosen, pot, pot_out, own,
    load_sem, walk_send, walk_recv, halo_send, halo_recv, pick_send, pick_recv,
    bias_send, bias_recv, shift_send, shift_recv, pot_send, pot_recv,
):
    me = lax.axis_index("pair")
    w_local, orbitals, occupied = walkers.shape
    rows = orbitals // count
    total = count * w_local
    vectors, pairs = chol.shape
    part = pairs // chunks
    per_part = rows // chunks
    tall = rows // pot_out.shape[0]

    def peer(k):
        return lax.rem(me + k, count)

    def remote(src, dst, send, recv, target):
        return pltpu.make_async_remote_copy(
            src_ref=src, dst_ref=dst, send_sem=send, recv_sem=recv,
            device_id={"pair": target}, device_id_type=MESH,
        )

    def load(c):
        columns = pl.ds(pl.multiple_of(c * part, part), part)
        return pltpu.make_async_copy(chol.at[:, columns], held.at[:, columns], load_sem.at[c])

    def each(low, high, body):
        lax.fori_loop(low, high, lambda k, carry: (body(k), carry)[1], 0)

    each(0, chunks, lambda c: load(c).start())

    barrier = pltpu.get_barrier_semaphore()
    each(1, count, lambda k: pl.semaphore_signal(
        barrier, inc=1, device_id={"pair": peer(k)}, device_id_type=MESH))
    pl.semaphore_wait(barrier, count - 1)

    def block(d):
        return pl.ds(pl.multiple_of(d * rows, rows), rows)

    def walk_copy(k):
        return remote(walkers.at[:, block(peer(k)), :], rows_in.at[me], walk_send.at[k], walk_recv.at[k], peer(k))

    def pick_copy(k):
        return remote(onehot, picks_in.at[me], pick_send.at[k], pick_recv.at[k], peer(k))

    def halo_copy(side):
        target = peer(1) if side == 0 else peer(count - 1)
        return remote(walkers, halo.at[side], halo_send.at[side], halo_recv.at[side], target)

    each(1, count, lambda k: walk_copy(k).start())
    each(1, count, lambda k: pick_copy(k).start())
    halo_copy(0).start()
    halo_copy(1).start()
    rows_in[me] = walkers[:, block(me), :]
    picks_in[me] = onehot[...]
    each(1, count, lambda k: walk_copy(k).wait())

    arrived = rows_in[...].astype(jnp.float32).reshape(total, rows, occupied)
    by_row = jnp.swapaxes(arrived, 0, 1).astype(jnp.bfloat16).reshape(rows * total, occupied)
    green[...] = lax.dot_general(
        by_row, trial[...], (((1,), (1,)), ((), ())), preferred_element_type=jnp.float32
    ).astype(jnp.bfloat16).reshape(rows, total, orbitals)

    def bias_part(c, acc):
        load(c).wait()
        for r in range(per_part):
            i = c * per_part + r
            acc = acc + lax.dot_general(
                green[i], held[:, pl.ds(pl.multiple_of(i * orbitals, orbitals), orbitals)],
                (((1,), (1,)), ((), ())), preferred_element_type=jnp.float32,
            )
        return acc

    acc = lax.fori_loop(0, chunks, bias_part, jnp.zeros((total, vectors), jnp.float32))
    for d in range(count):
        bias_out[d] = acc[d * w_local:(d + 1) * w_local]

    def bias_copy(k):
        return remote(bias_out.at[peer(k)], bias_in.at[me], bias_send.at[k], bias_recv.at[k], peer(k))

    each(1, count, lambda k: bias_copy(k).start())
    bias_in[me] = bias_out[me]
    each(1, count, lambda k: bias_copy(k).wait())
    summed = jnp.sum(bias_in[...], axis=0)
    shift = fields[...] - jnp.clip(sqrt_tau * summed, -bias_cap, bias_cap)
    shift_in[me] = shift.astype(jnp.bfloat16).astype(jnp.float32)

    def shift_copy(k):
        return remote(shift_in.at[me], shift_in.at[me], shift_send.at[k], shift_recv.at[k], peer(k))

    each(1, count, lambda k: shift_copy(k).start())
    each(1, count, lambda k: pick_copy(k).wait())
    flat[...] = jnp.zeros_like(flat)
    for d in range(count):
        picks[d * w_local:(d + 1) * w_local, :] = picks_in[d, 0:w_local, :]
    each(1, count, lambda k: shift_copy(k).wait())
    for d in range(count):
        flat[d * w_local:(d + 1) * w_local, :] = shift_in[d]
    chosen[...] = jnp.dot(
        picks[...].astype(jnp.bfloat16), flat[...].astype(jnp.bfloat16),
        preferred_element_type=jnp.float32,
    ).astype(jnp.bfloat16)

    def pot_copy(c, k):
        d = peer(k)
        return remote(
            pot_out.at[c, pl.ds(d * w_local, w_local)],
            own.at[:, pl.ds(pl.multiple_of(me * rows + c * tall, tall), tall), :],
            pot_send.at[c, k], pot_recv.at[c, k], d,
        )

    for c in range(rows // tall):
        def one_row(i):
            columns = pl.ds(pl.multiple_of((c * tall + i) * orbitals, orbitals), orbitals)
            pot[i] = sqrt_tau * jnp.dot(chosen[...], held[:, columns], preferred_element_type=jnp.float32)

        each(0, tall, one_row)
        for q in range(0, orbitals, 128):
            pot_out[c, :, :, q:q + 128] = jnp.swapaxes(pot[:, :, q:q + 128], 0, 1).astype(jnp.bfloat16)
        each(1, count, lambda k: pot_copy(c, k).start())
        own[:, pl.ds(pl.multiple_of(me * rows + c * tall, tall), tall), :] = pot_out[c, pl.ds(me * w_local, w_local)]

    halo_copy(0).wait()
    halo_copy(1).wait()
    near = (halo.at[0], walkers, halo.at[1])
    parents = []
    for j in range(w_local):
        parent = jnp.zeros((orbitals, occupied), jnp.float32)
        for s in range(3 * w_local):
            n = j * 3 * w_local + s
            parent = parent + weights[n:n + 1, :] * near[s // w_local][s % w_local].astype(jnp.float32)
        parents.append(parent)
    for c in range(rows // tall):
        each(1, count, lambda k: pot_copy(c, k).wait())
    for j in range(w_local):
        amat = (own[j].astype(jnp.float32) + one_body[...].astype(jnp.float32)).astype(jnp.bfloat16)
        term = parents[j].astype(jnp.bfloat16)
        result = parents[j]
        for order in range(1, TERMS):
            product = jnp.dot(amat, term, preferred_element_type=jnp.float32) / order
            result = result + product
            term = product.astype(jnp.bfloat16)
        out[j] = result.astype(jnp.bfloat16)


def shards(chol, walkers, trial, one_body, fields, src_shift, src_slot):
    w_local, orbitals, occupied = walkers.shape
    vectors, pairs = chol.shape
    count = lax.axis_size("pair")
    rows = orbitals // count
    total = count * w_local
    if rows % 16 or total > 128 or total % 16 or occupied != 128 or orbitals % 128 or w_local > 4:
        return plain_shards(chol, walkers, trial, one_body, fields, src_shift, src_slot)
    chunks = 8
    tall = 16
    me = lax.axis_index("pair")
    source = (me + src_shift + count) % count * w_local + src_slot
    onehot = (source[:, None] == jnp.arange(128)[None, :]).astype(jnp.float32)
    onehot = jnp.pad(onehot, ((0, 8 - w_local), (0, 0)))
    place = (src_shift + 1) * w_local + src_slot
    weights = (place[:, None] == jnp.arange(3 * w_local)[None, :]).astype(jnp.float32).reshape(-1, 1)
    weights = jnp.broadcast_to(weights, (weights.shape[0], 128))
    vmem = pl.BlockSpec(memory_space=pltpu.VMEM)
    dma = pltpu.SemaphoreType.DMA
    bf16, f32 = jnp.bfloat16, jnp.float32
    return pl.pallas_call(
        functools.partial(step_kernel, count, chunks),
        out_shape=jax.ShapeDtypeStruct(walkers.shape, bf16),
        in_specs=[pl.BlockSpec(memory_space=pl.ANY)] + [vmem] * 6,
        out_specs=vmem,
        scratch_shapes=[
            pltpu.VMEM((vectors, pairs), bf16),
            pltpu.VMEM((count, w_local, rows, occupied), bf16),
            pltpu.VMEM((2,) + walkers.shape, bf16),
            pltpu.VMEM((rows, total, orbitals), bf16),
            pltpu.VMEM((count, 8, 128), f32),
            pltpu.VMEM((count, w_local, vectors), f32),
            pltpu.VMEM((count, w_local, vectors), f32),
            pltpu.VMEM((count, w_local, vectors), f32),
            pltpu.VMEM((128, vectors), f32),
            pltpu.VMEM((total, 128), f32),
            pltpu.VMEM((total, vectors), bf16),
            pltpu.VMEM((tall, total, orbitals), f32),
            pltpu.VMEM((rows // tall, total, tall, orbitals), bf16),
            pltpu.VMEM((w_local, orbitals, orbitals), bf16),
            dma((chunks,)),
            dma((count,)), dma((count,)), dma((2,)), dma((2,)), dma((count,)), dma((count,)),
            dma((count,)), dma((count,)), dma((count,)), dma((count,)),
            dma((rows // tall, count)), dma((rows // tall, count)),
        ],
        compiler_params=pltpu.CompilerParams(
            collective_id=0, has_side_effects=True, vmem_limit_bytes=52 * 2**20
        ),
        cost_estimate=pl.CostEstimate(
            flops=4 * total * vectors * pairs, bytes_accessed=2 * vectors * pairs, transcendentals=0
        ),
    )(chol, walkers, trial, one_body, fields, onehot, weights)


def solution(mesh):
    placed = (
        P("groups", "pair"),
        P(("groups", "pair"), None, None),
        P("groups", None),
        P("groups", None),
        P(("groups", "pair"), None),
        P(("groups", "pair")),
        P(("groups", "pair")),
    )
    return jax.shard_map(
        shards,
        mesh=mesh,
        in_specs=placed,
        out_specs=P(("groups", "pair"), None, None),
        check_vma=False,
    )
```

```python
import functools

import jax
import jax.numpy as jnp
from jax import lax
from jax.experimental import pallas as pl
from jax.experimental.pallas import tpu as pltpu
from jax.sharding import PartitionSpec as P

TERMS = 6


sqrt_tau = 0.1
bias_cap = 1.0


def padded_2(block, sides, width):
    for axis, dim in sides:
        count = lax.axis_size(axis)
        forward = [(i, i + 1) for i in range(count - 1)]
        forward.append((count - 1, 0))
        backward = [(target, source) for source, target in forward]
        low = lax.ppermute(
            lax.slice_in_dim(block, block.shape[dim] - width, None, axis=dim), axis, forward
        )
        high = lax.ppermute(lax.slice_in_dim(block, 0, width, axis=dim), axis, backward)
        block = jnp.concatenate([low, block, high], axis=dim)
    return block


def taylor(amat, block):
    term = block
    total = block.astype(jnp.float32)
    for order in range(1, TERMS):
        product = jnp.einsum("wik,wka->wia", amat, term, preferred_element_type=jnp.float32) / order
        total = total + product
        term = product.astype(jnp.bfloat16)
    return total.astype(jnp.bfloat16)


def plain_shards(chol, walkers, trial, one_body, fields, src_shift, src_slot):
    w_local, orbitals, _ = walkers.shape
    count = lax.axis_size("pair")
    me = lax.axis_index("pair")
    moved = lax.all_to_all(walkers, "pair", split_axis=1, concat_axis=0, tiled=True)
    source = (me + src_shift + count) % count * w_local + src_slot
    sources = lax.all_gather(source, "pair", axis=0, tiled=True)
    padded = padded_2(walkers, (("pair", 0),), w_local)
    parents = jnp.take(padded, (src_shift + 1) * w_local + src_slot, axis=0)
    formed = jnp.einsum("wia,ka->wik", moved, trial, preferred_element_type=jnp.float32)
    green_rows = formed.astype(jnp.bfloat16).reshape(moved.shape[0], moved.shape[1] * orbitals)
    partial_bias = lax.dot_general(
        green_rows, chol, (((1,), (1,)), ((), ())), preferred_element_type=jnp.float32
    )
    pieces = lax.all_to_all(
        partial_bias.reshape(count, w_local, -1), "pair", split_axis=0, concat_axis=0, tiled=True
    )
    summed = jnp.sum(pieces, axis=0)
    shift = (fields - jnp.clip(sqrt_tau * summed, -bias_cap, bias_cap)).astype(jnp.bfloat16)
    spread = jnp.broadcast_to(shift[None], (count,) + shift.shape)
    every_shift = lax.all_to_all(spread, "pair", split_axis=0, concat_axis=0, tiled=True)
    chosen = jnp.take(every_shift.reshape(count * w_local, -1), sources, axis=0)
    local_potential = (sqrt_tau * jnp.dot(chosen, chol, preferred_element_type=jnp.float32)).astype(
        jnp.bfloat16
    )
    own_potential = lax.all_to_all(local_potential, "pair", split_axis=0, concat_axis=1, tiled=True)
    amat = own_potential.astype(jnp.float32).reshape(w_local, orbitals, orbitals) + one_body.astype(
        jnp.float32
    )
    return taylor(amat.astype(jnp.bfloat16), parents)


MESH = pl.DeviceIdType.MESH


def step_kernel(
    count, chunks, tall,
    chol, walkers_in, trial_in, body_in, fields, onehot, weights, out,
    walkers, trial, one_body, held, rows_in, halo, green, picks_in, bias_out, bias_in, shift_in, flat, picks,
    chosen, pot, pot_out, own,
    input_sem, load_sem, walk_send, walk_recv, halo_send, halo_recv, pick_send, pick_recv,
    bias_send, bias_recv, shift_send, shift_recv, first_send, first_recv, later_send, later_recv,
):
    me = lax.axis_index("pair")
    w_local, orbitals, occupied = walkers.shape
    rows = orbitals // count
    total = count * w_local
    vectors, pairs = chol.shape
    halves = rows // tall
    part = pairs // chunks
    per_part = rows // chunks

    def peer(k):
        return lax.rem(me + k, count)

    def remote(src, dst, send, recv, target):
        return pltpu.make_async_remote_copy(
            src_ref=src, dst_ref=dst, send_sem=send, recv_sem=recv,
            device_id={"pair": target}, device_id_type=MESH,
        )

    def load(c):
        columns = pl.ds(pl.multiple_of(c * part, part), part)
        return pltpu.make_async_copy(chol.at[:, columns], held.at[:, columns], load_sem.at[c])

    def each(low, high, body):
        lax.fori_loop(low, high, lambda k, carry: (body(k), carry)[1], 0)

    def partners(body):
        def one(j):
            body(count // 2 + (2 * lax.rem(j, 2) - 1) * (j // 2))

        each(1, count, one)

    inputs = [
        pltpu.make_async_copy(source, target, input_sem.at[n])
        for n, (source, target) in enumerate(
            ((walkers_in, walkers), (trial_in, trial), (body_in, one_body)))
    ]
    inputs[0].start()
    inputs[1].start()
    each(0, chunks, lambda c: load(c).start())
    inputs[2].start()

    barrier = pltpu.get_barrier_semaphore()
    each(1, count, lambda k: pl.semaphore_signal(
        barrier, inc=1, device_id={"pair": peer(k)}, device_id_type=MESH))
    pl.semaphore_wait(barrier, count - 1)

    def block(d, h):
        return pl.ds(pl.multiple_of(d * rows + h * tall, tall), tall)

    def walk_copy(h, k):
        return remote(
            walkers_in.at[:, block(peer(k), h), :], rows_in.at[h, me],
            walk_send.at[h, k], walk_recv.at[h, k], peer(k),
        )

    def pick_copy(k):
        return remote(onehot, picks_in.at[me], pick_send.at[k], pick_recv.at[k], peer(k))

    def halo_copy(side):
        target = peer(1) if side == 0 else peer(count - 1)
        return remote(walkers_in, halo.at[side], halo_send.at[side], halo_recv.at[side], target)

    for h in range(halves):
        partners(lambda k: walk_copy(h, k).start())
    inputs[0].wait()
    inputs[1].wait()
    for h in range(halves):
        rows_in[h, me] = walkers[:, block(me, h), :]
    picks_in[me] = onehot[...]

    def bias_part(c, acc):
        load(c).wait()
        for r in range(per_part):
            i = c * per_part + r
            acc = acc + lax.dot_general(
                green[i], held[:, pl.ds(pl.multiple_of(i * orbitals, orbitals), orbitals)],
                (((1,), (1,)), ((), ())), preferred_element_type=jnp.float32,
            )
        return acc

    acc = jnp.zeros((total, vectors), jnp.float32)
    for h in range(halves):
        partners(lambda k: walk_copy(h, k).wait())
        if h == halves - 1:
            partners(lambda k: pick_copy(k).start())
            halo_copy(0).start()
            halo_copy(1).start()
        arrived = rows_in[h].astype(jnp.float32).reshape(total, tall, occupied)
        by_row = jnp.swapaxes(arrived, 0, 1).astype(jnp.bfloat16).reshape(tall * total, occupied)
        green[h * tall:(h + 1) * tall] = lax.dot_general(
            by_row, trial[...], (((1,), (1,)), ((), ())), preferred_element_type=jnp.float32
        ).astype(jnp.bfloat16).reshape(tall, total, orbitals)
        acc = lax.fori_loop(h * chunks // halves, (h + 1) * chunks // halves, bias_part, acc)
    for d in range(count):
        bias_out[d] = acc[d * w_local:(d + 1) * w_local]

    def bias_copy(k):
        return remote(bias_out.at[peer(k)], bias_in.at[me], bias_send.at[k], bias_recv.at[k], peer(k))

    partners(lambda k: bias_copy(k).start())
    bias_in[me] = bias_out[me]
    each(1, count, lambda k: bias_copy(k).wait())
    summed = jnp.sum(bias_in[...], axis=0)
    shift = fields[...] - jnp.clip(sqrt_tau * summed, -bias_cap, bias_cap)
    shift_in[me] = shift.astype(jnp.bfloat16).astype(jnp.float32)

    def shift_copy(k):
        return remote(shift_in.at[me], shift_in.at[me], shift_send.at[k], shift_recv.at[k], peer(k))

    partners(lambda k: shift_copy(k).start())
    each(1, count, lambda k: pick_copy(k).wait())
    flat[...] = jnp.zeros_like(flat)
    for d in range(count):
        picks[d * w_local:(d + 1) * w_local, :] = picks_in[d, 0:w_local, :]
    each(1, count, lambda k: shift_copy(k).wait())
    for d in range(count):
        flat[d * w_local:(d + 1) * w_local, :] = shift_in[d]
    chosen[...] = jnp.dot(
        picks[...].astype(jnp.bfloat16), flat[...].astype(jnp.bfloat16),
        preferred_element_type=jnp.float32,
    ).astype(jnp.bfloat16)

    wide = orbitals // 2

    def first_copy(n, k):
        c, q = n // 2, n % 2 * wide
        d = peer(k)
        return remote(
            pot_out.at[d * w_local, c * tall:(c + 1) * tall, q:q + wide],
            own.at[0, block(me, c), q:q + wide],
            first_send.at[n, k], first_recv.at[n, k], d,
        )

    def later_copy(slot, k):
        d = peer(k)
        return remote(
            pot_out.at[d * w_local + slot],
            own.at[slot, pl.ds(pl.multiple_of(me * rows, rows), rows), :],
            later_send.at[slot, k], later_recv.at[slot, k], d,
        )

    for n in range(2 * halves):
        c, q = n // 2, n % 2 * wide

        def one_row(i):
            columns = pl.ds(pl.multiple_of((c * tall + i) * orbitals + q, wide), wide)
            pot[i] = sqrt_tau * jnp.dot(chosen[...], held[:, columns], preferred_element_type=jnp.float32)

        each(0, tall, one_row)
        for p in range(0, wide, 128):
            pot_out[:, c * tall:(c + 1) * tall, q + p:q + p + 128] = jnp.swapaxes(
                pot[:, :, p:p + 128], 0, 1).astype(jnp.bfloat16)
        partners(lambda k: first_copy(n, k).start())
    for slot in range(1, w_local):
        partners(lambda k: later_copy(slot, k).start())
    for slot in range(w_local):
        own[slot, pl.ds(pl.multiple_of(me * rows, rows), rows), :] = pot_out[me * w_local + slot]

    halo_copy(0).wait()
    halo_copy(1).wait()
    near = (halo.at[0], walkers, halo.at[1])
    parents = []
    for j in range(w_local):
        parent = jnp.zeros((orbitals, occupied), jnp.float32)
        for s in range(3 * w_local):
            n = j * 3 * w_local + s
            parent = parent + weights[n:n + 1, :] * near[s // w_local][s % w_local].astype(jnp.float32)
        parents.append(parent)
    inputs[2].wait()
    for j in range(w_local):
        if j == 0:
            for n in range(2 * halves):
                partners(lambda k: first_copy(n, k).wait())
        else:
            partners(lambda k: later_copy(j, k).wait())
        amat = (own[j].astype(jnp.float32) + one_body[...].astype(jnp.float32)).astype(jnp.bfloat16)
        term = parents[j].astype(jnp.bfloat16)
        result = parents[j]
        for order in range(1, TERMS):
            product = jnp.dot(amat, term, preferred_element_type=jnp.float32) / order
            result = result + product
            term = product.astype(jnp.bfloat16)
        out[j] = result.astype(jnp.bfloat16)


def shards(chol, walkers, trial, one_body, fields, src_shift, src_slot):
    w_local, orbitals, occupied = walkers.shape
    vectors, pairs = chol.shape
    count = lax.axis_size("pair")
    rows = orbitals // count
    total = count * w_local
    if rows % 16 or 8 % max(rows // 16, 1) or count % 2 or total > 128 or total % 16 or occupied != 128 or orbitals % 256 or w_local > 4:
        return plain_shards(chol, walkers, trial, one_body, fields, src_shift, src_slot)
    chunks = 8
    tall = 16
    me = lax.axis_index("pair")
    source = (me + src_shift + count) % count * w_local + src_slot
    onehot = (source[:, None] == jnp.arange(128)[None, :]).astype(jnp.float32)
    onehot = jnp.pad(onehot, ((0, 8 - w_local), (0, 0)))
    place = (src_shift + 1) * w_local + src_slot
    weights = (place[:, None] == jnp.arange(3 * w_local)[None, :]).astype(jnp.float32).reshape(-1, 1)
    weights = jnp.broadcast_to(weights, (weights.shape[0], 128))
    vmem = pl.BlockSpec(memory_space=pltpu.VMEM)
    dma = pltpu.SemaphoreType.DMA
    bf16, f32 = jnp.bfloat16, jnp.float32
    return pl.pallas_call(
        functools.partial(step_kernel, count, chunks, tall),
        out_shape=jax.ShapeDtypeStruct(walkers.shape, bf16),
        in_specs=[pl.BlockSpec(memory_space=pl.ANY)] * 4 + [vmem] * 3,
        out_specs=vmem,
        scratch_shapes=[
            pltpu.VMEM(walkers.shape, bf16),
            pltpu.VMEM(trial.shape, bf16),
            pltpu.VMEM(one_body.shape, bf16),
            pltpu.VMEM((vectors, pairs), bf16),
            pltpu.VMEM((rows // tall, count, w_local, tall, occupied), bf16),
            pltpu.VMEM((2,) + walkers.shape, bf16),
            pltpu.VMEM((rows, total, orbitals), bf16),
            pltpu.VMEM((count, 8, 128), f32),
            pltpu.VMEM((count, w_local, vectors), f32),
            pltpu.VMEM((count, w_local, vectors), f32),
            pltpu.VMEM((count, w_local, vectors), f32),
            pltpu.VMEM((128, vectors), f32),
            pltpu.VMEM((total, 128), f32),
            pltpu.VMEM((total, vectors), bf16),
            pltpu.VMEM((tall, total, orbitals // 2), f32),
            pltpu.VMEM((total, rows, orbitals), bf16),
            pltpu.VMEM((w_local, orbitals, orbitals), bf16),
            dma((3,)), dma((chunks,)),
            dma((rows // tall, count)), dma((rows // tall, count)), dma((2,)), dma((2,)), dma((count,)), dma((count,)),
            dma((count,)), dma((count,)), dma((count,)), dma((count,)),
            dma((2 * rows // tall, count)), dma((2 * rows // tall, count)),
            dma((w_local, count)), dma((w_local, count)),
        ],
        compiler_params=pltpu.CompilerParams(
            collective_id=0, has_side_effects=True, vmem_limit_bytes=52 * 2**20
        ),
        cost_estimate=pl.CostEstimate(
            flops=4 * total * vectors * pairs, bytes_accessed=2 * vectors * pairs, transcendentals=0
        ),
    )(chol, walkers, trial, one_body, fields, onehot, weights)


def solution(mesh):
    placed = (
        P("groups", "pair"),
        P(("groups", "pair"), None, None),
        P("groups", None),
        P("groups", None),
        P(("groups", "pair"), None),
        P(("groups", "pair")),
        P(("groups", "pair")),
    )
    return jax.shard_map(
        shards,
        mesh=mesh,
        in_specs=placed,
        out_specs=P(("groups", "pair"), None, None),
        check_vma=False,
    )
```

```python
import functools

import jax
import jax.numpy as jnp
from jax import lax
from jax.experimental import pallas as pl
from jax.experimental.pallas import tpu as pltpu
from jax.sharding import PartitionSpec as P

TERMS = 6


sqrt_tau = 0.1
bias_cap = 1.0


def padded_2(block, sides, width):
    for axis, dim in sides:
        count = lax.axis_size(axis)
        forward = [(i, i + 1) for i in range(count - 1)]
        forward.append((count - 1, 0))
        backward = [(target, source) for source, target in forward]
        low = lax.ppermute(
            lax.slice_in_dim(block, block.shape[dim] - width, None, axis=dim), axis, forward
        )
        high = lax.ppermute(lax.slice_in_dim(block, 0, width, axis=dim), axis, backward)
        block = jnp.concatenate([low, block, high], axis=dim)
    return block


def taylor(amat, block):
    term = block
    total = block.astype(jnp.float32)
    for order in range(1, TERMS):
        product = jnp.einsum("wik,wka->wia", amat, term, preferred_element_type=jnp.float32) / order
        total = total + product
        term = product.astype(jnp.bfloat16)
    return total.astype(jnp.bfloat16)


def plain_shards(chol, walkers, trial, one_body, fields, src_shift, src_slot):
    w_local, orbitals, _ = walkers.shape
    count = lax.axis_size("pair")
    me = lax.axis_index("pair")
    moved = lax.all_to_all(walkers, "pair", split_axis=1, concat_axis=0, tiled=True)
    source = (me + src_shift + count) % count * w_local + src_slot
    sources = lax.all_gather(source, "pair", axis=0, tiled=True)
    padded = padded_2(walkers, (("pair", 0),), w_local)
    parents = jnp.take(padded, (src_shift + 1) * w_local + src_slot, axis=0)
    formed = jnp.einsum("wia,ka->wik", moved, trial, preferred_element_type=jnp.float32)
    green_rows = formed.astype(jnp.bfloat16).reshape(moved.shape[0], moved.shape[1] * orbitals)
    partial_bias = lax.dot_general(
        green_rows, chol, (((1,), (1,)), ((), ())), preferred_element_type=jnp.float32
    )
    pieces = lax.all_to_all(
        partial_bias.reshape(count, w_local, -1), "pair", split_axis=0, concat_axis=0, tiled=True
    )
    summed = jnp.sum(pieces, axis=0)
    shift = (fields - jnp.clip(sqrt_tau * summed, -bias_cap, bias_cap)).astype(jnp.bfloat16)
    spread = jnp.broadcast_to(shift[None], (count,) + shift.shape)
    every_shift = lax.all_to_all(spread, "pair", split_axis=0, concat_axis=0, tiled=True)
    chosen = jnp.take(every_shift.reshape(count * w_local, -1), sources, axis=0)
    local_potential = (sqrt_tau * jnp.dot(chosen, chol, preferred_element_type=jnp.float32)).astype(
        jnp.bfloat16
    )
    own_potential = lax.all_to_all(local_potential, "pair", split_axis=0, concat_axis=1, tiled=True)
    amat = own_potential.astype(jnp.float32).reshape(w_local, orbitals, orbitals) + one_body.astype(
        jnp.float32
    )
    return taylor(amat.astype(jnp.bfloat16), parents)


SPLITS = 2
UNROLL = 16
MESH = pl.DeviceIdType.MESH


def step_kernel(
    count, chunks, tall,
    chol, walkers_in, trial_in, body_in, fields, onehot, weights, out,
    walkers, trial, one_body, held, rows_in, halo, green, picks_in, bias_out, bias_in, shift_in, flat, picks,
    chosen, pot, pot_out, own,
    input_sem, load_sem, walk_send, walk_recv, halo_send, halo_recv, pick_send, pick_recv,
    bias_send, bias_recv, shift_send, shift_recv, first_send, first_recv, later_send, later_recv,
):
    me = lax.axis_index("pair")
    w_local, orbitals, occupied = walkers.shape
    rows = orbitals // count
    total = count * w_local
    vectors, pairs = chol.shape
    halves = rows // tall
    part = pairs // chunks
    per_part = rows // chunks

    def peer(k):
        return lax.rem(me + k, count)

    def remote(src, dst, send, recv, target):
        return pltpu.make_async_remote_copy(
            src_ref=src, dst_ref=dst, send_sem=send, recv_sem=recv,
            device_id={"pair": target}, device_id_type=MESH,
        )

    def load(c):
        columns = pl.ds(pl.multiple_of(c * part, part), part)
        return pltpu.make_async_copy(chol.at[:, columns], held.at[:, columns], load_sem.at[c])

    def each(low, high, body):
        lax.fori_loop(low, high, lambda k, carry: (body(k), carry)[1], 0)

    def partners(body):
        def one(j):
            body(count // 2 + (2 * lax.rem(j, 2) - 1) * (j // 2))

        each(1, count, one)

    inputs = [
        pltpu.make_async_copy(source, target, input_sem.at[n])
        for n, (source, target) in enumerate(
            ((walkers_in, walkers), (trial_in, trial), (body_in, one_body)))
    ]
    inputs[0].start()
    inputs[1].start()
    each(0, chunks, lambda c: load(c).start())
    inputs[2].start()

    barrier = pltpu.get_barrier_semaphore()
    each(1, count, lambda k: pl.semaphore_signal(
        barrier, inc=1, device_id={"pair": peer(k)}, device_id_type=MESH))
    pl.semaphore_wait(barrier, count - 1)

    def block(d, h):
        return pl.ds(pl.multiple_of(d * rows + h * tall, tall), tall)

    def walk_copy(h, k):
        return remote(
            walkers_in.at[:, block(peer(k), h), :], rows_in.at[h, me],
            walk_send.at[h, k], walk_recv.at[h, k], peer(k),
        )

    def pick_copy(k):
        return remote(onehot, picks_in.at[me], pick_send.at[k], pick_recv.at[k], peer(k))

    def halo_copy(side):
        target = peer(1) if side == 0 else peer(count - 1)
        return remote(walkers_in, halo.at[side], halo_send.at[side], halo_recv.at[side], target)

    for h in range(halves):
        partners(lambda k: walk_copy(h, k).start())
    inputs[0].wait()
    inputs[1].wait()
    for h in range(halves):
        rows_in[h, me] = walkers[:, block(me, h), :]
    picks_in[me] = onehot[...]

    def bias_part(c, acc):
        load(c).wait()
        for r in range(per_part):
            i = c * per_part + r
            acc = acc + lax.dot_general(
                green[i], held[:, pl.ds(pl.multiple_of(i * orbitals, orbitals), orbitals)],
                (((1,), (1,)), ((), ())), preferred_element_type=jnp.float32,
            )
        return acc

    acc = jnp.zeros((total, vectors), jnp.float32)
    for h in range(halves):
        partners(lambda k: walk_copy(h, k).wait())
        if h == halves - 1:
            partners(lambda k: pick_copy(k).start())
            halo_copy(0).start()
            halo_copy(1).start()
        arrived = rows_in[h].astype(jnp.float32).reshape(total, tall, occupied)
        by_row = jnp.swapaxes(arrived, 0, 1).astype(jnp.bfloat16).reshape(tall * total, occupied)
        green[h * tall:(h + 1) * tall] = lax.dot_general(
            by_row, trial[...], (((1,), (1,)), ((), ())), preferred_element_type=jnp.float32
        ).astype(jnp.bfloat16).reshape(tall, total, orbitals)
        acc = lax.fori_loop(h * chunks // halves, (h + 1) * chunks // halves, bias_part, acc)
    for d in range(count):
        for q in range(vectors // 128):
            bias_out[d, q * w_local:(q + 1) * w_local, :] = acc[d * w_local:(d + 1) * w_local, q * 128:(q + 1) * 128]

    def bias_copy(k):
        return remote(bias_out.at[peer(k)], bias_in.at[me], bias_send.at[k], bias_recv.at[k], peer(k))

    partners(lambda k: bias_copy(k).start())
    bias_in[me] = bias_out[me]
    each(1, count, lambda k: bias_copy(k).wait())
    summed = jnp.sum(bias_in[...], axis=0)
    shift = fields[...] - jnp.clip(sqrt_tau * summed, -bias_cap, bias_cap)
    shift_in[me] = shift.astype(jnp.bfloat16)

    def shift_copy(k):
        return remote(shift_in.at[me], shift_in.at[me], shift_send.at[k], shift_recv.at[k], peer(k))

    partners(lambda k: shift_copy(k).start())
    each(1, count, lambda k: pick_copy(k).wait())
    flat[...] = jnp.zeros_like(flat)
    for d in range(count):
        picks[d * w_local:(d + 1) * w_local, :] = picks_in[d, 0:w_local, :]
    each(1, count, lambda k: shift_copy(k).wait())
    for d in range(count):
        one_shift = shift_in[d].astype(jnp.float32)
        for q in range(vectors // 128):
            flat[d * w_local:(d + 1) * w_local, q * 128:(q + 1) * 128] = one_shift[q * w_local:(q + 1) * w_local, :]
    chosen[...] = jnp.dot(
        picks[...].astype(jnp.bfloat16), flat[...].astype(jnp.bfloat16),
        preferred_element_type=jnp.float32,
    ).astype(jnp.bfloat16)

    wide = orbitals // SPLITS

    def first_copy(n, k):
        c, q = n // SPLITS, n % SPLITS * wide
        d = peer(k)
        return remote(
            pot_out.at[d * w_local, c * tall:(c + 1) * tall, q:q + wide],
            own.at[0, block(me, c), q:q + wide],
            first_send.at[n, k], first_recv.at[n, k], d,
        )

    def later_copy(slot, k):
        d = peer(k)
        return remote(
            pot_out.at[d * w_local + slot],
            own.at[slot, pl.ds(pl.multiple_of(me * rows, rows), rows), :],
            later_send.at[slot, k], later_recv.at[slot, k], d,
        )

    for n in range(SPLITS * halves):
        c, q = n // SPLITS, n % SPLITS * wide

        def some_rows(g):
            for u in range(UNROLL):
                i = g * UNROLL + u
                columns = pl.ds(pl.multiple_of((c * tall + i) * orbitals + q, wide), wide)
                pot[i] = sqrt_tau * jnp.dot(chosen[...], held[:, columns], preferred_element_type=jnp.float32)

        each(0, tall // UNROLL, some_rows)
        for p in range(0, wide, 128):
            pot_out[:, c * tall:(c + 1) * tall, q + p:q + p + 128] = jnp.swapaxes(
                pot[:, :, p:p + 128], 0, 1).astype(jnp.bfloat16)
        partners(lambda k: first_copy(n, k).start())
    for slot in range(1, w_local):
        partners(lambda k: later_copy(slot, k).start())
    for slot in range(w_local):
        own[slot, pl.ds(pl.multiple_of(me * rows, rows), rows), :] = pot_out[me * w_local + slot]

    halo_copy(0).wait()
    halo_copy(1).wait()
    near = (halo.at[0], walkers, halo.at[1])
    parents = []
    for j in range(w_local):
        parent = jnp.zeros((orbitals, occupied), jnp.float32)
        for s in range(3 * w_local):
            n = j * 3 * w_local + s
            parent = parent + weights[n:n + 1, :] * near[s // w_local][s % w_local].astype(jnp.float32)
        parents.append(parent)
    inputs[2].wait()
    for j in range(w_local):
        if j == 0:
            for n in range(SPLITS * halves):
                partners(lambda k: first_copy(n, k).wait())
        else:
            partners(lambda k: later_copy(j, k).wait())
        amat = (own[j].astype(jnp.float32) + one_body[...].astype(jnp.float32)).astype(jnp.bfloat16)
        term = parents[j].astype(jnp.bfloat16)
        result = parents[j]
        for order in range(1, TERMS):
            product = jnp.dot(amat, term, preferred_element_type=jnp.float32) / order
            result = result + product
            term = product.astype(jnp.bfloat16)
        out[j] = result.astype(jnp.bfloat16)


def shards(chol, walkers, trial, one_body, fields, src_shift, src_slot):
    w_local, orbitals, occupied = walkers.shape
    vectors, pairs = chol.shape
    count = lax.axis_size("pair")
    rows = orbitals // count
    total = count * w_local
    if rows % 16 or vectors % 128 or (w_local * vectors // 128) % 16 or 8 % max(rows // 16, 1) or count % 2 or total > 128 or total % 16 or occupied != 128 or orbitals % 256 or w_local > 4:
        return plain_shards(chol, walkers, trial, one_body, fields, src_shift, src_slot)
    chunks = 8
    tall = 16
    me = lax.axis_index("pair")
    source = (me + src_shift + count) % count * w_local + src_slot
    onehot = (source[:, None] == jnp.arange(128)[None, :]).astype(jnp.float32)
    onehot = jnp.pad(onehot, ((0, 8 - w_local), (0, 0)))
    place = (src_shift + 1) * w_local + src_slot
    weights = (place[:, None] == jnp.arange(3 * w_local)[None, :]).astype(jnp.float32).reshape(-1, 1)
    weights = jnp.broadcast_to(weights, (weights.shape[0], 128))
    tiles = w_local * vectors // 128
    laid = fields.reshape(w_local, vectors // 128, 128).swapaxes(0, 1).reshape(tiles, 128)
    vmem = pl.BlockSpec(memory_space=pltpu.VMEM)
    dma = pltpu.SemaphoreType.DMA
    bf16, f32 = jnp.bfloat16, jnp.float32
    return pl.pallas_call(
        functools.partial(step_kernel, count, chunks, tall),
        out_shape=jax.ShapeDtypeStruct(walkers.shape, bf16),
        in_specs=[pl.BlockSpec(memory_space=pl.ANY)] * 4 + [vmem] * 3,
        out_specs=vmem,
        scratch_shapes=[
            pltpu.VMEM(walkers.shape, bf16),
            pltpu.VMEM(trial.shape, bf16),
            pltpu.VMEM(one_body.shape, bf16),
            pltpu.VMEM((vectors, pairs), bf16),
            pltpu.VMEM((rows // tall, count, w_local, tall, occupied), bf16),
            pltpu.VMEM((2,) + walkers.shape, bf16),
            pltpu.VMEM((rows, total, orbitals), bf16),
            pltpu.VMEM((count, 8, 128), f32),
            pltpu.VMEM((count, tiles, 128), f32),
            pltpu.VMEM((count, tiles, 128), f32),
            pltpu.VMEM((count, tiles, 128), bf16),
            pltpu.VMEM((128, vectors), f32),
            pltpu.VMEM((total, 128), f32),
            pltpu.VMEM((total, vectors), bf16),
            pltpu.VMEM((tall, total, orbitals // SPLITS), f32),
            pltpu.VMEM((total, rows, orbitals), bf16),
            pltpu.VMEM((w_local, orbitals, orbitals), bf16),
            dma((3,)), dma((chunks,)),
            dma((rows // tall, count)), dma((rows // tall, count)), dma((2,)), dma((2,)), dma((count,)), dma((count,)),
            dma((count,)), dma((count,)), dma((count,)), dma((count,)),
            dma((SPLITS * rows // tall, count)), dma((SPLITS * rows // tall, count)),
            dma((w_local, count)), dma((w_local, count)),
        ],
        compiler_params=pltpu.CompilerParams(
            collective_id=0, has_side_effects=True, vmem_limit_bytes=52 * 2**20
        ),
        cost_estimate=pl.CostEstimate(
            flops=4 * total * vectors * pairs, bytes_accessed=2 * vectors * pairs, transcendentals=0
        ),
    )(chol, walkers, trial, one_body, laid, onehot, weights)


def solution(mesh):
    placed = (
        P("groups", "pair"),
        P(("groups", "pair"), None, None),
        P("groups", None),
        P("groups", None),
        P(("groups", "pair"), None),
        P(("groups", "pair")),
        P(("groups", "pair")),
    )
    return jax.shard_map(
        shards,
        mesh=mesh,
        in_specs=placed,
        out_specs=P(("groups", "pair"), None, None),
        check_vma=False,
    )
```
